512 devices in a mesh: frame: 64 (over z_hi, y, x, core), head: 8 (over z_lo).
Axes of the slice: x: 4, y: 4, z: 16 (z_hi: 2, z_lo: 8; z = z_hi * 8 + z_lo), core: 2. Of those that a mesh axis runs over, the one named last changes fastest.
Arguments:
- latents: bfloat16 [64, 512, 3072], P('frame', 'head'), may hold values from -4 to 4
- queries: bfloat16 [64, 512, 3072], P('frame', 'head'), may hold values from -25 to 25
- keys: bfloat16 [64, 512, 3072], P('frame', 'head'), may hold values from -25 to 25
- values: bfloat16 [64, 512, 3072], P('frame', 'head'), may hold values from -6 to 6
- fresh: bfloat16 [512, 3072], P('head'), may hold values from -6 to 6
- timesteps: int32 [64], P('frame'), may hold values from 0 to 999
- window: int32 [64, 2], P('frame'), may hold values from 0 to 2, as said below
Outputs:
- denoised: bfloat16 [64, 512, 3072], P('frame', 'head')
- queue: bfloat16 [64, 512, 3072], P('frame', 'head')
The draws below stay inside these ranges and needn't reach their ends.
Inputs may be any that keep to these rules, and one draw needn't show every extreme that they name: `window`: frame 64 - 1 has column 0 equal to 2; some frame has column 1 equal to 0.
All inputs are finite; a program needn't handle non-finite values.
Results may differ from the reference program's by a relative error of at most 0.012.
Values may be sent and summed in bfloat16 or wider, within the bound.
No kernel may reach another device: no remote copies, remote signals or barrier semaphores. Data moves between devices by JAX's collectives and lax.ppermute only.
A program may use at most 64 MiB of HBM per device.

```python
import jax
import jax.numpy as jnp
from jax import lax

HEADS = 48
HD = 64
D = 3072
TOKF = 512
REACH = 2
LEVELS = 1000
FRAMES = 64


def draw_queries(key, part):
    key = jax.random.fold_in(key, 11)
    result = 2.5 * jnp.clip(jax.random.normal(key, (FRAMES, TOKF, D), jnp.float32), -4.0, 4.0)
    return result.astype(jnp.bfloat16)


def draw_keys(key, part):
    key = jax.random.fold_in(key, 13)
    result = jnp.clip(jax.random.normal(key, (FRAMES, TOKF, D), jnp.float32), -4.0, 4.0)
    return result.astype(jnp.bfloat16)


def draw_window(key, part):
    key = jax.random.fold_in(key, 23)
    reach_key, chosen_key = jax.random.split(key)
    spans = jax.random.randint(reach_key, (FRAMES, 2), 0, REACH + 1)
    chosen = jax.random.randint(chosen_key, (2,), 0, FRAMES)
    spans = spans.at[chosen[0], 0].set(REACH)
    spans = spans.at[chosen[1], 1].set(0)
    spans = spans.at[FRAMES - 1, 0].set(REACH)
    return spans.astype(jnp.int32)


def touch_ends(entries, rng, low, top_value):
    shape = entries.shape
    index_at = [jax.random.randint(jax.random.fold_in(rng, axis), (), 0, shape[axis]) for axis in range(len(shape))]
    entries = entries.at[tuple(index_at)].set(low)
    longest = shape.index(max(shape))
    index_at[longest] = (index_at[longest] + 1) % shape[longest]
    return entries.at[tuple(index_at)].set(top_value)


def steps_of(own_key, extent, shards, smallest, high):
    factor_of = 1.0
    for axis_at, parts in shards:
        steps = jax.random.uniform(jax.random.fold_in(jax.random.fold_in(own_key, 6), axis_at), (parts,), jnp.float32, smallest / len(shards), high / len(shards))
        factor_of = factor_of * jnp.repeat(jnp.exp(steps), extent[axis_at] // parts).reshape((-1,) + (1,) * (len(extent) - 1 - axis_at))
    return factor_of


def gaussian(rng, shape, width, most, cuts=(), held_as=jnp.bfloat16):
    values = jax.random.normal(rng, shape, jnp.float32) * width
    if len(cuts) > 0:
        values = steps_of(rng, shape, cuts, -0.22, 0.18) * values
    return jnp.clip(values, min=-most, max=most).astype(held_as)


def setup_inputs(seed: int = 0) -> dict:
    key_of = jax.random.split(jax.random.key(seed), 8)
    latents = gaussian(key_of[0], (FRAMES, TOKF, D), 0.3, 4.0, ((0, 64), (1, 8)))
    queries = draw_queries(jax.random.fold_in(key_of[7], 71), 0)
    keys = draw_keys(jax.random.fold_in(key_of[7], 71), 0)
    values = gaussian(key_of[3], (FRAMES, TOKF, D), 1.0, 6.0, ((0, 64), (1, 8)))
    fresh = gaussian(key_of[4], (TOKF, D), 1.0, 6.0, ((0, 8),))
    timesteps = touch_ends(jax.random.randint(key_of[5], (FRAMES,), 0, LEVELS), jax.random.fold_in(key_of[5], 1), 0, LEVELS - 1).astype(jnp.int32)
    window = draw_window(jax.random.fold_in(key_of[7], 71), 0)
    return {"latents": latents, "queries": queries, "keys": keys, "values": values, "fresh": fresh, "timesteps": timesteps, "window": window}


def frame_attention(frame, queries, keys, values, window):
    offsets = jnp.arange(-REACH, REACH + 1).astype(jnp.int32)
    target = frame + offsets
    allowed = (target >= 0) & (target < FRAMES) & (offsets >= -window[frame, 0]) & (offsets <= window[frame, 1])
    clipped = jnp.clip(target, 0, FRAMES - 1).astype(jnp.int32)
    key_rows = keys[clipped].reshape(-1, HEADS, HD).astype(jnp.float32)
    value_rows = values[clipped].reshape(-1, HEADS, HD).astype(jnp.float32)
    query_rows = queries[frame].reshape(TOKF, HEADS, HD).astype(jnp.float32)
    scores = jnp.einsum("qhd,khd->hqk", query_rows, key_rows) * (HD ** -0.5)
    usable = jnp.repeat(allowed, TOKF)
    scores = jnp.where(usable[None, None, :], scores, -jnp.inf)
    highest = jnp.max(scores, axis=2, keepdims=True)
    weights = jnp.exp(scores - highest)
    weights = (weights / jnp.sum(weights, axis=2, keepdims=True)).astype(jnp.bfloat16)
    mixed = jnp.einsum("hqk,khd->qhd", weights.astype(jnp.float32), value_rows)
    return mixed.astype(jnp.bfloat16).reshape(TOKF, HEADS * HD)


def reference(latents, queries, keys, values, fresh, timesteps, window):
    def one_frame(frame):
        return frame_attention(frame, queries, keys, values, window)

    attended = lax.map(one_frame, jnp.arange(FRAMES).astype(jnp.int32))
    levels = timesteps.astype(jnp.float32) / LEVELS
    keep_share = (1.0 - 0.5 * levels)[:, None, None]
    push_share = (0.5 + levels)[:, None, None]
    denoised = (keep_share * latents.astype(jnp.float32) + push_share * attended.astype(jnp.float32)).astype(jnp.bfloat16)
    return (denoised, jnp.concatenate([fresh[None], denoised[:-1]], axis=0))
```

```python
import functools

import jax
import jax.numpy as jnp
from jax import lax
from jax.experimental import pallas as pl
from jax.experimental.pallas import tpu as pltpu
from jax.sharding import PartitionSpec as P

HD = 64
REACH = 2
LEVELS = 1000
SLOTS = 2 * REACH + 1
PAIR = 2 * HD
LOG2E = 1.4426950408889634
AXES = ("frame", "head")


def head_split_kernel(groups, width, flip_ref, *refs):
    inputs, out_ref, sem = refs[:-2], refs[-2], refs[-1]
    flip = flip_ref[0]
    copies = []
    for block in range(groups):
        group = jnp.where(flip == 1, groups - 1 - block, block)
        columns = pl.ds(pl.multiple_of(group * width, 128), width)
        for index, source in enumerate(inputs):
            copies.append(
                pltpu.make_async_copy(source.at[:, columns], out_ref.at[block, index], sem.at[block, index])
            )
    for copy in copies:
        copy.start()
    for copy in copies:
        copy.wait()


def head_split(flip, groups, *arrays):
    rows, columns = arrays[0].shape
    width = columns // groups
    count = len(arrays)
    size = count * rows * columns * 2
    return pl.pallas_call(
        functools.partial(head_split_kernel, groups, width),
        out_shape=jax.ShapeDtypeStruct((groups, count, rows, width), jnp.bfloat16),
        in_specs=[pl.BlockSpec(memory_space=pltpu.SMEM)] + [pl.BlockSpec(memory_space=pl.ANY)] * count,
        out_specs=pl.BlockSpec(memory_space=pl.ANY),
        scratch_shapes=[pltpu.SemaphoreType.DMA((groups, count))],
        cost_estimate=pl.CostEstimate(flops=0, bytes_accessed=2 * size, transcendentals=0),
    )(flip, *arrays)


def attention_kernel(
    blocks, pairs, rows, picks_ref, q_ref, own, back2, back1, next1, next2, cross, cross_near,
    out_ref, k_buf, v_buf, score, high, total, sem,
):
    per_block = own.shape[2]
    span = blocks * per_block

    def copies(source, slot, pair):
        found = []
        for which, buf in enumerate((k_buf, v_buf)):
            for block in range(blocks):
                found.append(
                    pltpu.make_async_copy(
                        source.at[block, which, :, pl.ds(pair * PAIR, PAIR)],
                        buf.at[pair, slot, pl.ds(block * per_block, per_block), pl.ds(0, PAIR)],
                        sem.at[pair, slot],
                    )
                )
        return found

    sources = (back2, back1, own, next1, next2)
    crossing = (cross, cross_near, None, cross_near, cross)
    for pair in range(pairs):
        for slot in range(SLOTS):
            @pl.when(picks_ref[slot] == 1)
            def _(pair=pair, slot=slot):
                for copy in copies(sources[slot], slot, pair):
                    copy.start()

            if crossing[slot] is not None:
                @pl.when(picks_ref[slot] == 2)
                def _(pair=pair, slot=slot):
                    for copy in copies(crossing[slot], slot, pair):
                        copy.start()

    v_buf[:, :, :, PAIR:] = jnp.ones((pairs, SLOTS, span, PAIR), jnp.bfloat16)
    lane = lax.broadcasted_iota(jnp.int32, (rows, PAIR), 1)
    for pair in range(pairs):
        for slot in range(SLOTS):
            @pl.when(picks_ref[slot] > 0)
            def _(pair=pair, slot=slot):
                for copy in copies(sources[slot], slot, pair):
                    copy.wait()

        for chunk in range(span // rows):
            per_chunk = rows // per_block
            query = q_ref[chunk * per_chunk : (chunk + 1) * per_chunk, 0, :, pair * PAIR : (pair + 1) * PAIR]
            query = query.reshape(rows, PAIR)
            zero = jnp.zeros_like(query)
            both = jnp.concatenate(
                [jnp.where(lane < HD, query, zero), jnp.where(lane < HD, zero, query)], axis=0
            )
            high[...] = jnp.full(high.shape, -jnp.inf, jnp.float32)
            total[...] = jnp.zeros(total.shape, jnp.float32)
            for slot in range(SLOTS):
                @pl.when(picks_ref[slot] > 0)
                def _(pair=pair, slot=slot):
                    found = lax.dot_general(
                        both, k_buf[pair, slot], (((1,), (1,)), ((), ())), preferred_element_type=jnp.float32
                    )
                    score[slot] = found
                    high[...] = jnp.maximum(high[...], jnp.max(found, axis=1, keepdims=True))
            for slot in range(SLOTS):
                @pl.when(picks_ref[slot] > 0)
                def _(pair=pair, slot=slot):
                    weights = jnp.exp2((score[slot] - high[...]) * (HD ** -0.5 * LOG2E)).astype(jnp.bfloat16)
                    total[...] += jnp.dot(weights, v_buf[pair, slot], preferred_element_type=jnp.float32)
            mixed = total[:, :PAIR] / total[:, PAIR:]
            mixed = jnp.where(lane < HD, mixed[:rows], mixed[rows:]).astype(jnp.bfloat16)
            out_ref[chunk * per_chunk : (chunk + 1) * per_chunk, :, pair * PAIR : (pair + 1) * PAIR] = mixed.reshape(
                per_chunk, per_block, PAIR
            )


def attend(picks, query, own, back2, back1, next1, next2, cross, cross_near):
    blocks, _, per_block, width = query.shape
    pairs = width // PAIR
    span = blocks * per_block
    rows = 256
    return pl.pallas_call(
        functools.partial(attention_kernel, blocks, pairs, rows),
        out_shape=jax.ShapeDtypeStruct((blocks, per_block, width), jnp.bfloat16),
        in_specs=[pl.BlockSpec(memory_space=pltpu.SMEM), pl.BlockSpec(memory_space=pltpu.VMEM)]
        + [pl.BlockSpec(memory_space=pl.ANY)] * 7,
        out_specs=pl.BlockSpec(memory_space=pltpu.VMEM),
        scratch_shapes=[
            pltpu.VMEM((pairs, SLOTS, span, PAIR), jnp.bfloat16),
            pltpu.VMEM((pairs, SLOTS, span, 2 * PAIR), jnp.bfloat16),
            pltpu.VMEM((SLOTS, 2 * rows, span), jnp.float32),
            pltpu.VMEM((2 * rows, 1), jnp.float32),
            pltpu.VMEM((2 * rows, 2 * PAIR), jnp.float32),
            pltpu.SemaphoreType.DMA((pairs, SLOTS)),
        ],
        compiler_params=pltpu.CompilerParams(vmem_limit_bytes=40 * 1024 * 1024),
        cost_estimate=pl.CostEstimate(
            flops=4 * span * span * SLOTS * width,
            bytes_accessed=(2 * SLOTS + 2) * span * width * 2,
            transcendentals=span * span * SLOTS * width // HD,
        ),
    )(picks, query, own, back2, back1, next1, next2, cross, cross_near)


def blend_kernel(groups, width, flip_ref, share_ref, latents_ref, returned_ref, out_ref):
    flip = flip_ref[0]
    for group in range(groups):
        block = jnp.where(flip == 1, groups - 1 - group, group)
        columns = slice(group * width, (group + 1) * width)
        out_ref[:, columns] = (
            share_ref[0] * latents_ref[:, columns].astype(jnp.float32)
            + share_ref[1] * returned_ref[block].astype(jnp.float32)
        ).astype(jnp.bfloat16)


def blend(flip, shares, latents, returned):
    groups, rows, width = returned.shape
    return pl.pallas_call(
        functools.partial(blend_kernel, groups, width),
        out_shape=jax.ShapeDtypeStruct(latents.shape, jnp.bfloat16),
        in_specs=[pl.BlockSpec(memory_space=pltpu.SMEM)] * 2 + [pl.BlockSpec(memory_space=pltpu.VMEM)] * 2,
        out_specs=pl.BlockSpec(memory_space=pltpu.VMEM),
        cost_estimate=pl.CostEstimate(flops=3 * latents.size, bytes_accessed=6 * latents.size, transcendentals=0),
    )(flip, shares, latents, returned)


def per_device(frames, heads, latents, queries, keys, values, fresh, timesteps, window):
    frame = lax.axis_index("frame")
    half = frames // 2
    flip = (frame >= half).astype(jnp.int32)[None]

    def mirrored(moves):
        return [
            (a * heads + z, b * heads + (heads - 1 - z)) for a, b in moves for z in range(heads)
        ]

    def straight(moves):
        return [(a * heads + z, b * heads + z) for a, b in moves for z in range(heads)]

    def within(distance):
        return straight(
            [(f, f + distance) for f in range(frames) if 0 <= f + distance < frames and (f < half) == (f + distance < half)]
        )

    send = lambda value, moves: lax.ppermute(value, AXES, moves)
    exchange = lambda value: lax.all_to_all(value, "head", split_axis=0, concat_axis=0, tiled=True)

    own = exchange(head_split(flip, heads, keys, values))
    query = head_split(flip, heads, queries)
    own, query = lax.optimization_barrier((own, query))

    mid = heads // 2
    cross_a = send(own[:mid], mirrored([(half - 2, half), (half - 1, half + 1), (half + 1, half - 1), (half, half - 2)]))
    relay = send(
        own[mid:], straight([(half - 2, half - 4), (half - 1, half - 3), (half + 1, half + 3), (half, half + 2)])
    )
    cross_b = send(relay, mirrored([(half - 4, half), (half - 3, half + 1), (half + 3, half - 1), (half + 2, half - 2)]))
    back2 = send(own, within(2))
    next2 = send(own, within(-2))
    back1 = send(own, within(1))
    next1 = send(own, within(-1))
    cross = jnp.concatenate([cross_a, cross_b])
    cross_near = send(cross, straight([(half + 1, half), (half - 2, half - 1)]))

    query = exchange(query)

    offsets = jnp.arange(-REACH, REACH + 1)
    target = frame + offsets
    allowed = (
        (target >= 0) & (target < frames) & (offsets >= -window[0, 0]) & (offsets <= window[0, 1])
    )
    picks = jnp.where(allowed, jnp.where((target < half) == (frame < half), 1, 2), 0).astype(jnp.int32)
    attended = attend(picks, query, own, back2, back1, next1, next2, cross, cross_near)
    returned = exchange(attended)
    levels = timesteps.astype(jnp.float32) / LEVELS
    shares = jnp.concatenate([1.0 - 0.5 * levels, 0.5 + levels])
    denoised = blend(flip, shares, latents[0], returned)[None]
    advanced = send(denoised, straight([(f, f + 1) for f in range(frames - 1)]))
    return (denoised, jnp.where(frame == 0, fresh[None], advanced))


def solution(mesh):
    def body(latents, queries, keys, values, fresh, timesteps, window):
        return per_device(
            mesh.shape["frame"], mesh.shape["head"], latents, queries[0], keys[0], values[0], fresh, timesteps, window
        )

    return jax.shard_map(
        body,
        mesh=mesh,
        in_specs=(
            P("frame", "head", None),
            P("frame", "head", None),
            P("frame", "head", None),
            P("frame", "head", None),
            P("head", None),
            P("frame"),
            P("frame", None),
        ),
        out_specs=(P("frame", "head", None), P("frame", "head", None)),
        check_vma=False,
    )
```

```python
import functools

import jax
import jax.numpy as jnp
from jax import lax
from jax.experimental import pallas as pl
from jax.experimental.pallas import tpu as pltpu
from jax.sharding import PartitionSpec as P

HD = 64
REACH = 2
LEVELS = 1000
SLOTS = 2 * REACH + 1
PAIR = 2 * HD
LOG2E = 1.4426950408889634
AXES = ("frame", "head")
EXITS_A = ((2, 3), (3, 2), (3, 2), (3, 3))
EXITS_B = ((0, 3), (3, 0), (3, 0), (3, 3))
EXITS_STEP = ((3, 3), (3, 2), (3, 0), (2, 3), (0, 3), (3, 3), (3, 2), (3, 0))


def head_split_kernel(groups, width, flip_ref, *refs):
    inputs, out_ref = refs[:-1], refs[-1]
    flip = flip_ref[0]
    for group in range(groups):
        block = jnp.where(flip == 1, groups - 1 - group, group)
        for index, source in enumerate(inputs):
            out_ref[block, index] = source[:, group * width : (group + 1) * width]


def head_split(flip, groups, *arrays):
    rows, columns = arrays[0].shape
    width = columns // groups
    count = len(arrays)
    size = count * rows * columns * 2
    return pl.pallas_call(
        functools.partial(head_split_kernel, groups, width),
        out_shape=jax.ShapeDtypeStruct((groups, count, rows, width), jnp.bfloat16),
        in_specs=[pl.BlockSpec(memory_space=pltpu.SMEM)] + [pl.BlockSpec(memory_space=pltpu.VMEM)] * count,
        out_specs=pl.BlockSpec(memory_space=pltpu.VMEM),
        cost_estimate=pl.CostEstimate(flops=0, bytes_accessed=2 * size, transcendentals=0),
    )(flip, *arrays)


def attention_kernel(
    blocks, pairs, rows, picks_ref, q_ref, own, back2, next2, cross, chip, far,
    out_ref, k_buf, v_buf, score_a, score_b, sem,
):
    per_block = own.shape[2]
    span = blocks * per_block
    per_chunk = rows // per_block
    chunks = span // rows
    steps = pairs * chunks

    def copies(source, slot, pair, which, buf):
        columns = pl.ds(pair * PAIR, PAIR)
        return [
            pltpu.make_async_copy(
                source.at[block, which, :, columns],
                buf.at[pair, slot, pl.ds(block * per_block, per_block), pl.ds(0, PAIR)],
                sem.at[pair, slot, which],
            )
            for block in range(blocks)
        ]

    def fetch(source, slot, pair):
        for copy in copies(source, slot, pair, 0, k_buf) + copies(source, slot, pair, 1, v_buf):
            copy.start()

    sources = (back2, chip, own, chip, next2)
    others = (cross, far, None, far, cross)
    for pair in range(pairs):
        for slot in range(SLOTS):
            if slot == REACH:
                fetch(own, slot, pair)
                continue

            @pl.when(picks_ref[slot] == 0)
            def _(pair=pair, slot=slot):
                for copy in copies(own, slot, pair, 0, k_buf):
                    copy.start()
                v_buf[pair, slot] = jnp.zeros((span, 2 * PAIR), jnp.bfloat16)

            @pl.when(picks_ref[slot] == 1)
            def _(pair=pair, slot=slot):
                fetch(sources[slot], slot, pair)

            @pl.when(picks_ref[slot] == 2)
            def _(pair=pair, slot=slot):
                fetch(others[slot], slot, pair)

    for pair in range(pairs):
        for slot in range(SLOTS):
            @pl.when(picks_ref[slot] > 0)
            def _(pair=pair, slot=slot):
                v_buf[pair, slot, :, PAIR:] = jnp.ones((span, PAIR), jnp.bfloat16)

    def arrive(pair):
        for slot in range(SLOTS):
            for copy in copies(own, slot, pair, 0, k_buf):
                copy.wait()

            @pl.when(picks_ref[slot] > 0)
            def _(slot=slot):
                for copy in copies(own, slot, pair, 1, v_buf):
                    copy.wait()

    lane = lax.broadcasted_iota(jnp.int32, (rows, PAIR), 1)

    def place(step):
        pair, chunk = step // chunks, step % chunks
        return pl.ds(chunk * per_chunk, per_chunk), pl.ds(pl.multiple_of(pair * PAIR, PAIR), PAIR)

    def scores(step, score):
        block, columns = place(step)
        query = q_ref[block, 0, :, columns].reshape(rows, PAIR)
        zero = jnp.zeros_like(query)
        both = jnp.concatenate([jnp.where(lane < HD, query, zero), jnp.where(lane < HD, zero, query)], axis=0)
        high = None
        for slot in range(SLOTS):
            found = lax.dot_general(
                both, k_buf[step // chunks, slot], (((1,), (1,)), ((), ())), preferred_element_type=jnp.float32
            )
            score[slot] = found
            for start in range(0, span, 128):
                part = found[:, start : start + 128]
                high = part if high is None else jnp.maximum(high, part)
        return jnp.max(high, axis=1, keepdims=True)

    def mix(step, score, high):
        total = None
        for slot in range(SLOTS):
            weights = jnp.exp2((score[slot] - high) * (HD ** -0.5 * LOG2E)).astype(jnp.bfloat16)
            part = jnp.dot(weights, v_buf[step // chunks, slot], preferred_element_type=jnp.float32)
            total = part if total is None else total + part
        mixed = total[:, :PAIR] / total[:, PAIR:]
        mixed = jnp.where(lane < HD, mixed[:rows], mixed[rows:]).astype(jnp.bfloat16)
        block, columns = place(step)
        out_ref[block, :, columns] = mixed.reshape(per_chunk, per_block, PAIR)

    arrive(0)
    first = scores(0, score_a)

    def two_steps(index, high_a):
        later = jnp.minimum(2 * index + 2, steps - 1)
        high_b = scores(2 * index + 1, score_b)
        mix(2 * index, score_a, high_a)
        for pair in range(1, pairs):
            @pl.when(2 * index + 2 == pair * chunks)
            def _(pair=pair):
                arrive(pair)

        high_a = scores(later, score_a)
        mix(2 * index + 1, score_b, high_b)
        return high_a

    lax.fori_loop(0, steps // 2, two_steps, first)


def attend(picks, query, own, back2, next2, cross, chip, far):
    blocks, _, per_block, width = query.shape
    pairs = width // PAIR
    span = blocks * per_block
    rows = span // 2
    return pl.pallas_call(
        functools.partial(attention_kernel, blocks, pairs, rows),
        out_shape=jax.ShapeDtypeStruct((blocks, per_block, width), jnp.bfloat16),
        in_specs=[pl.BlockSpec(memory_space=pltpu.SMEM), pl.BlockSpec(memory_space=pltpu.VMEM)]
        + [pl.BlockSpec(memory_space=pl.ANY)] * 6,
        out_specs=pl.BlockSpec(memory_space=pltpu.VMEM),
        scratch_shapes=[
            pltpu.VMEM((pairs, SLOTS, span, PAIR), jnp.bfloat16),
            pltpu.VMEM((pairs, SLOTS, span, 2 * PAIR), jnp.bfloat16),
            pltpu.VMEM((SLOTS, 2 * rows, span), jnp.float32),
            pltpu.VMEM((SLOTS, 2 * rows, span), jnp.float32),
            pltpu.SemaphoreType.DMA((pairs, SLOTS, 2)),
        ],
        compiler_params=pltpu.CompilerParams(vmem_limit_bytes=40 * 1024 * 1024),
        cost_estimate=pl.CostEstimate(
            flops=4 * span * span * SLOTS * width,
            bytes_accessed=(2 * SLOTS + 2) * span * width * 2,
            transcendentals=span * span * SLOTS * width // HD,
        ),
    )(picks, query, own, back2, next2, cross, chip, far)


def blend_kernel(groups, width, flip_ref, share_ref, latents_ref, returned_ref, out_ref):
    flip = flip_ref[0]
    for group in range(groups):
        block = jnp.where(flip == 1, groups - 1 - group, group)
        columns = slice(group * width, (group + 1) * width)
        out_ref[:, columns] = (
            share_ref[0] * latents_ref[:, columns].astype(jnp.float32)
            + share_ref[1] * returned_ref[block].astype(jnp.float32)
        ).astype(jnp.bfloat16)


def blend(flip, shares, latents, returned):
    groups, rows, width = returned.shape
    return pl.pallas_call(
        functools.partial(blend_kernel, groups, width),
        out_shape=jax.ShapeDtypeStruct(latents.shape, jnp.bfloat16),
        in_specs=[pl.BlockSpec(memory_space=pltpu.SMEM)] * 2 + [pl.BlockSpec(memory_space=pltpu.VMEM)] * 2,
        out_specs=pl.BlockSpec(memory_space=pltpu.VMEM),
        cost_estimate=pl.CostEstimate(flops=3 * latents.size, bytes_accessed=6 * latents.size, transcendentals=0),
    )(flip, shares, latents, returned)


def per_device(frames, heads, latents, queries, keys, values, fresh, timesteps, window):
    frame = lax.axis_index("frame")
    half = frames // 2
    flip = (frame >= half).astype(jnp.int32)[None]

    def mirrored(moves):
        return [
            (a * heads + z, b * heads + (heads - 1 - z)) for a, b in moves for z in range(heads)
        ]

    def straight(moves):
        return [(a * heads + z, b * heads + z) for a, b in moves for z in range(heads)]

    def within(distance):
        return straight(
            [(f, f + distance) for f in range(frames) if 0 <= f + distance < frames and (f < half) == (f + distance < half)]
        )

    send = lambda value, moves: lax.ppermute(value, AXES, moves)
    exchange = lambda value: lax.all_to_all(value, "head", split_axis=0, concat_axis=0, tiled=True)

    own = exchange(head_split(flip, heads, keys, values))
    query = head_split(flip, heads, queries)
    own, query = lax.optimization_barrier((own, query))

    mid = heads // 2
    edge = (half - 2, half - 1, half, half + 1)
    over = {half - 2: half, half - 1: half + 1, half: half - 2, half + 1: half - 1}

    def column(f, z, exits):
        x, y = exits[min(z, heads - 1 - z)]
        ahead = y * 8 + x * 2 + f % 2
        return ahead if f < half else frames - 2 - ahead + 2 * (f % 2)

    def through(value, exits):
        out = [(f * heads + z, column(f, z, exits) * heads + z) for f in edge for z in range(heads)]
        on = [
            (column(f, z, exits) * heads + z, over[f] * heads + heads - 1 - z) for f in edge for z in range(heads)
        ]
        return send(value, out), on

    near_a, on_a = through(own[:mid], EXITS_A)
    near_b, on_b = through(own[mid:], EXITS_B)
    core = frame % 2
    pairwise = straight([(f, f ^ 1) for f in range(frames)])
    chip = send(own, pairwise)
    own, near_a, near_b = lax.optimization_barrier((own, near_a, near_b))
    back2 = send(own, within(2))
    next2 = send(own, within(-2))
    cross = jnp.concatenate([send(near_a, on_a), send(near_b, on_b)])
    fetched = jnp.where(core == 1, back2, next2)
    far = send(jnp.where((frame == half + 1) | (frame == half - 2), cross, fetched), pairwise)

    near_a, near_b, query = lax.optimization_barrier((near_a, near_b, query))
    query = exchange(query)

    offsets = jnp.arange(-REACH, REACH + 1)
    target = frame + offsets
    allowed = (
        (target >= 0) & (target < frames) & (offsets >= -window[0, 0]) & (offsets <= window[0, 1])
    )
    other = jnp.where(offsets % 2 == 0, (target < half) != (frame < half), target // 2 != frame // 2)
    picks = jnp.where(allowed, jnp.where(other, 2, 1), 0).astype(jnp.int32)
    attended = attend(picks, query, own, back2, next2, cross, chip, far)
    returned = exchange(attended)
    levels = timesteps.astype(jnp.float32) / LEVELS
    shares = jnp.concatenate([1.0 - 0.5 * levels, 0.5 + levels])
    denoised = blend(flip, shares, latents[0], returned)[None]

    def step_column(z):
        x, y = EXITS_STEP[z]
        return y * 8 + x * 2 + 1

    stepping = send(denoised, [((half - 1) * heads + z, step_column(z) * heads + z) for z in range(heads)])
    advanced = send(denoised, straight([(f, f + 1) for f in range(frames - 1) if f != half - 1]))
    stepped = send(stepping, [(step_column(z) * heads + z, half * heads + z) for z in range(heads)])
    advanced = jnp.where(frame == half, stepped, advanced)
    return (denoised, jnp.where(frame == 0, fresh[None], advanced))


def solution(mesh):
    def body(latents, queries, keys, values, fresh, timesteps, window):
        return per_device(
            mesh.shape["frame"], mesh.shape["head"], latents, queries[0], keys[0], values[0], fresh, timesteps, window
        )

    return jax.shard_map(
        body,
        mesh=mesh,
        in_specs=(
            P("frame", "head", None),
            P("frame", "head", None),
            P("frame", "head", None),
            P("frame", "head", None),
            P("head", None),
            P("frame"),
            P("frame", None),
        ),
        out_specs=(P("frame", "head", None), P("frame", "head", None)),
        check_vma=False,
    )
```

```python
import functools

import jax
import jax.numpy as jnp
from jax import lax
from jax.experimental import pallas as pl
from jax.experimental.pallas import tpu as pltpu
from jax.sharding import PartitionSpec as P

HD = 64
REACH = 2
LEVELS = 1000
SLOTS = 2 * REACH + 1
PAIR = 2 * HD
LOG2E = 1.4426950408889634
AXES = ("frame", "head")
EXITS_A = ((2, 3), (3, 2), (3, 2), (3, 3))
EXITS_B = ((0, 3), (3, 0), (3, 0), (3, 3))
EXITS_STEP = ((2, 2), (1, 3), (2, 0), (0, 0), (0, 2), (3, 1), (2, 0), (1, 3))
MARK_LENT = 2 * 10**9
MARK_PIECES = 16 * 10**9


def head_split_kernel(groups, width, flip_ref, *refs):
    inputs, out_ref = refs[:-1], refs[-1]
    flip = flip_ref[0]
    for group in range(groups):
        block = jnp.where(flip == 1, groups - 1 - group, group)
        for index, source in enumerate(inputs):
            out_ref[block, index] = source[:, group * width : (group + 1) * width]


def head_split(flip, groups, *arrays):
    rows, columns = arrays[0].shape
    width = columns // groups
    count = len(arrays)
    size = count * rows * columns * 2
    return pl.pallas_call(
        functools.partial(head_split_kernel, groups, width),
        out_shape=jax.ShapeDtypeStruct((groups, count, rows, width), jnp.bfloat16),
        in_specs=[pl.BlockSpec(memory_space=pltpu.SMEM)] + [pl.BlockSpec(memory_space=pltpu.VMEM)] * count,
        out_specs=pl.BlockSpec(memory_space=pltpu.VMEM),
        cost_estimate=pl.CostEstimate(flops=0, bytes_accessed=2 * size, transcendentals=0),
    )(flip, *arrays)


def attention_kernel(
    blocks, pairs, rows, picks_ref, q_ref, own, back2, next2, cross, chip, far,
    out_ref, k_buf, v_buf, score_a, score_b, sem,
):
    per_block = own.shape[2]
    span = blocks * per_block
    per_chunk = rows // per_block
    chunks = span // rows
    steps = pairs * chunks

    def copies(source, slot, pair, which, buf):
        columns = pl.ds(pair * PAIR, PAIR)
        return [
            pltpu.make_async_copy(
                source.at[block, which, :, columns],
                buf.at[pair, slot, pl.ds(block * per_block, per_block), pl.ds(0, PAIR)],
                sem.at[pair, slot, which],
            )
            for block in range(blocks)
        ]

    def fetch(source, slot, pair):
        for copy in copies(source, slot, pair, 0, k_buf) + copies(source, slot, pair, 1, v_buf):
            copy.start()

    sources = (back2, chip, own, chip, next2)
    others = (cross, far, None, far, cross)
    for pair in range(pairs):
        for slot in range(SLOTS):
            if slot == REACH:
                fetch(own, slot, pair)
                continue

            @pl.when(picks_ref[slot] == 0)
            def _(pair=pair, slot=slot):
                for copy in copies(own, slot, pair, 0, k_buf):
                    copy.start()
                v_buf[pair, slot] = jnp.zeros((span, 2 * PAIR), jnp.bfloat16)

            @pl.when(picks_ref[slot] == 1)
            def _(pair=pair, slot=slot):
                fetch(sources[slot], slot, pair)

            @pl.when(picks_ref[slot] == 2)
            def _(pair=pair, slot=slot):
                fetch(others[slot], slot, pair)

    for pair in range(pairs):
        for slot in range(SLOTS):
            @pl.when(picks_ref[slot] > 0)
            def _(pair=pair, slot=slot):
                v_buf[pair, slot, :, PAIR:] = jnp.ones((span, PAIR), jnp.bfloat16)

    def arrive(pair):
        for slot in range(SLOTS):
            for copy in copies(own, slot, pair, 0, k_buf):
                copy.wait()

            @pl.when(picks_ref[slot] > 0)
            def _(slot=slot):
                for copy in copies(own, slot, pair, 1, v_buf):
                    copy.wait()

    lane = lax.broadcasted_iota(jnp.int32, (rows, PAIR), 1)

    def place(step):
        pair, chunk = step // chunks, step % chunks
        return pl.ds(chunk * per_chunk, per_chunk), pl.ds(pl.multiple_of(pair * PAIR, PAIR), PAIR)

    def scores(step, score):
        block, columns = place(step)
        query = q_ref[block, 0, :, columns].reshape(rows, PAIR)
        zero = jnp.zeros_like(query)
        both = jnp.concatenate([jnp.where(lane < HD, query, zero), jnp.where(lane < HD, zero, query)], axis=0)
        high = None
        for slot in range(SLOTS):
            found = lax.dot_general(
                both, k_buf[step // chunks, slot], (((1,), (1,)), ((), ())), preferred_element_type=jnp.float32
            )
            score[slot] = found
            for start in range(0, span, 128):
                part = found[:, start : start + 128]
                high = part if high is None else jnp.maximum(high, part)
        return jnp.max(high, axis=1, keepdims=True)

    def mix(step, score, high):
        total = None
        for slot in range(SLOTS):
            weights = jnp.exp2((score[slot] - high) * (HD ** -0.5 * LOG2E)).astype(jnp.bfloat16)
            part = jnp.dot(weights, v_buf[step // chunks, slot], preferred_element_type=jnp.float32)
            total = part if total is None else total + part
        mixed = total[:, :PAIR] / total[:, PAIR:]
        mixed = jnp.where(lane < HD, mixed[:rows], mixed[rows:]).astype(jnp.bfloat16)
        block, columns = place(step)
        out_ref[block, :, columns] = mixed.reshape(per_chunk, per_block, PAIR)

    arrive(0)
    first = scores(0, score_a)

    def two_steps(index, high_a):
        later = jnp.minimum(2 * index + 2, steps - 1)
        high_b = scores(2 * index + 1, score_b)
        mix(2 * index, score_a, high_a)
        for pair in range(1, pairs):
            @pl.when(2 * index + 2 == pair * chunks)
            def _(pair=pair):
                arrive(pair)

        high_a = scores(later, score_a)
        mix(2 * index + 1, score_b, high_b)
        return high_a

    lax.fori_loop(0, steps // 2, two_steps, first)


def attend(picks, query, own, back2, next2, cross, chip, far):
    blocks, _, per_block, width = query.shape
    pairs = width // PAIR
    span = blocks * per_block
    rows = span // 2
    return pl.pallas_call(
        functools.partial(attention_kernel, blocks, pairs, rows),
        out_shape=jax.ShapeDtypeStruct((blocks, per_block, width), jnp.bfloat16),
        in_specs=[pl.BlockSpec(memory_space=pltpu.SMEM), pl.BlockSpec(memory_space=pltpu.VMEM)]
        + [pl.BlockSpec(memory_space=pl.ANY)] * 6,
        out_specs=pl.BlockSpec(memory_space=pltpu.VMEM),
        scratch_shapes=[
            pltpu.VMEM((pairs, SLOTS, span, PAIR), jnp.bfloat16),
            pltpu.VMEM((pairs, SLOTS, span, 2 * PAIR), jnp.bfloat16),
            pltpu.VMEM((SLOTS, 2 * rows, span), jnp.float32),
            pltpu.VMEM((SLOTS, 2 * rows, span), jnp.float32),
            pltpu.SemaphoreType.DMA((pairs, SLOTS, 2)),
        ],
        compiler_params=pltpu.CompilerParams(vmem_limit_bytes=40 * 1024 * 1024),
        cost_estimate=pl.CostEstimate(
            flops=4 * span * span * SLOTS * width,
            bytes_accessed=(2 * SLOTS + 2) * span * width * 2,
            transcendentals=span * span * SLOTS * width // HD,
        ),
    )(picks, query, own, back2, next2, cross, chip, far)


def blend_kernel(groups, width, flip_ref, share_ref, latents_ref, returned_ref, out_ref):
    flip = flip_ref[0]
    for group in range(groups):
        block = jnp.where(flip == 1, groups - 1 - group, group)
        columns = slice(group * width, (group + 1) * width)
        out_ref[:, columns] = (
            share_ref[0] * latents_ref[:, columns].astype(jnp.float32)
            + share_ref[1] * returned_ref[block].astype(jnp.float32)
        ).astype(jnp.bfloat16)


def blend(flip, shares, latents, returned):
    groups, rows, width = returned.shape
    return pl.pallas_call(
        functools.partial(blend_kernel, groups, width),
        out_shape=jax.ShapeDtypeStruct(latents.shape, jnp.bfloat16),
        in_specs=[pl.BlockSpec(memory_space=pltpu.SMEM)] * 2 + [pl.BlockSpec(memory_space=pltpu.VMEM)] * 2,
        out_specs=pl.BlockSpec(memory_space=pltpu.VMEM),
        cost_estimate=pl.CostEstimate(flops=3 * latents.size, bytes_accessed=6 * latents.size, transcendentals=0),
    )(flip, shares, latents, returned)


def mark_kernel(value_ref, out_ref):
    pass


def mark(value, flops):
    return pl.pallas_call(
        mark_kernel,
        out_shape=jax.ShapeDtypeStruct(value.shape, value.dtype),
        in_specs=[pl.BlockSpec(memory_space=pl.ANY)],
        out_specs=pl.BlockSpec(memory_space=pl.ANY),
        input_output_aliases={0: 0},
        compiler_params=pltpu.CompilerParams(vmem_limit_bytes=40 * 1024 * 1024),
        cost_estimate=pl.CostEstimate(flops=flops, bytes_accessed=0, transcendentals=0),
    )(value)


def blend_lent_kernel(groups, rows, width, order_ref, before_ref, returned_ref, fresh_ref, out_ref):
    first = order_ref[groups] == 1
    high = before_ref[rows : rows + 1, :width].astype(jnp.float32)
    low = before_ref[rows + 1 : rows + 2, :width].astype(jnp.float32)
    level = (high * 32.0 + low) / LEVELS
    keep_share = 1.0 - 0.5 * level
    push_share = 0.5 + level
    for group in range(groups):
        block = order_ref[group]
        columns = slice(group * width, (group + 1) * width)
        entry = (
            keep_share * before_ref[:rows, columns].astype(jnp.float32)
            + push_share * returned_ref[block].astype(jnp.float32)
        ).astype(jnp.bfloat16)
        out_ref[:, columns] = jnp.where(first, fresh_ref[:, columns], entry)


def blend_lent(order, before, returned, fresh):
    groups, rows, width = returned.shape
    shape = (rows, groups * width)
    return pl.pallas_call(
        functools.partial(blend_lent_kernel, groups, rows, width),
        out_shape=jax.ShapeDtypeStruct(shape, jnp.bfloat16),
        in_specs=[pl.BlockSpec(memory_space=pltpu.SMEM)] + [pl.BlockSpec(memory_space=pltpu.VMEM)] * 3,
        out_specs=pl.BlockSpec(memory_space=pltpu.VMEM),
        cost_estimate=pl.CostEstimate(
            flops=3 * rows * groups * width, bytes_accessed=6 * rows * groups * width, transcendentals=0
        ),
    )(order, before, returned, fresh)


def with_step(latents, timesteps):
    row = lax.broadcasted_iota(jnp.int32, (16, latents.shape[1]), 0)
    step = jnp.where(row == 0, timesteps[0] // 32, jnp.where(row == 1, timesteps[0] % 32, 0))
    return jnp.concatenate([latents, step.astype(jnp.bfloat16)])


def sort_kernel(parity_ref, *refs):
    pieces, kept_ref, given_ref = refs[:-2], refs[-2], refs[-1]
    parity = parity_ref[0]
    for index, piece in enumerate(pieces):
        kept_ref[index] = piece[parity]
        given_ref[index] = piece[1 - parity]


def sort_pieces(parity, pieces, flops):
    shape = jax.ShapeDtypeStruct((len(pieces), *pieces[0].shape[1:]), pieces[0].dtype)
    return pl.pallas_call(
        sort_kernel,
        out_shape=(shape, shape),
        in_specs=[pl.BlockSpec(memory_space=pltpu.SMEM)] + [pl.BlockSpec(memory_space=pltpu.VMEM)] * len(pieces),
        out_specs=(pl.BlockSpec(memory_space=pltpu.VMEM), pl.BlockSpec(memory_space=pltpu.VMEM)),
        cost_estimate=pl.CostEstimate(flops=flops, bytes_accessed=0, transcendentals=0),
    )(parity, *pieces)


def per_device(frames, heads, latents, queries, keys, values, fresh, timesteps, window):
    frame = lax.axis_index("frame")
    half = frames // 2
    flip = (frame >= half).astype(jnp.int32)[None]

    def mirrored(moves):
        return [
            (a * heads + z, b * heads + (heads - 1 - z)) for a, b in moves for z in range(heads)
        ]

    def straight(moves):
        return [(a * heads + z, b * heads + z) for a, b in moves for z in range(heads)]

    def within(distance):
        return straight(
            [(f, f + distance) for f in range(frames) if 0 <= f + distance < frames and (f < half) == (f + distance < half)]
        )

    send = lambda value, moves: lax.ppermute(value, AXES, moves)
    exchange = lambda value: lax.all_to_all(value, "head", split_axis=0, concat_axis=0, tiled=True)

    own = exchange(head_split(flip, heads, keys, values))
    query = head_split(flip, heads, queries)
    lent_to = [(y * 8 + x * 2 + 1) * heads + a for a, (x, y) in enumerate(EXITS_STEP)]
    lending = [((half - 1) * heads + a, lent_to[a]) for a in range(heads)]
    before = send(with_step(latents[0], timesteps), lending)
    own, query, before = lax.optimization_barrier((own, query, before))

    mid = heads // 2
    edge = (half - 2, half - 1, half, half + 1)
    over = {half - 2: half, half - 1: half + 1, half: half - 2, half + 1: half - 1}

    def column(f, z, exits):
        x, y = exits[min(z, heads - 1 - z)]
        ahead = y * 8 + x * 2 + f % 2
        return ahead if f < half else frames - 2 - ahead + 2 * (f % 2)

    def through(value, exits):
        out = [(f * heads + z, column(f, z, exits) * heads + z) for f in edge for z in range(heads)]
        on = [
            (column(f, z, exits) * heads + z, over[f] * heads + heads - 1 - z) for f in edge for z in range(heads)
        ]
        return send(value, out), on

    near_a, on_a = through(own[:mid], EXITS_A)
    near_b, on_b = through(own[mid:], EXITS_B)
    core = frame % 2
    pairwise = straight([(f, f ^ 1) for f in range(frames)])
    chip = send(own, pairwise)
    own, near_a, near_b = lax.optimization_barrier((own, near_a, near_b))
    back2 = send(own, within(2))
    next2 = send(own, within(-2))
    cross = jnp.concatenate([send(near_a, on_a), send(near_b, on_b)])
    fetched = jnp.where(core == 1, back2, next2)
    far = send(jnp.where((frame == half + 1) | (frame == half - 2), cross, fetched), pairwise)

    near_a, near_b, query = lax.optimization_barrier((near_a, near_b, query))
    query = exchange(query)

    offsets = jnp.arange(-REACH, REACH + 1)
    target = frame + offsets
    allowed = (
        (target >= 0) & (target < frames) & (offsets >= -window[0, 0]) & (offsets <= window[0, 1])
    )
    other = jnp.where(offsets % 2 == 0, (target < half) != (frame < half), target // 2 != frame // 2)
    picks = jnp.where(allowed, jnp.where(other, 2, 1), 0).astype(jnp.int32)
    attended = attend(picks, query, own, back2, next2, cross, chip, far)
    z = lax.axis_index("head")
    levels = timesteps.astype(jnp.float32) / LEVELS
    shares = jnp.concatenate([1.0 - 0.5 * levels, 0.5 + levels])
    attended, before = lax.optimization_barrier((attended, before))
    returned = exchange(attended)
    lent = attended.reshape(mid, 2, *attended.shape[1:])
    pieces = [
        send(
            lax.dynamic_index_in_dim(lent, (z // 2 + shift) % mid, 0, keepdims=False),
            [((half - 1) * heads + a, half * heads + (a + 2 * shift) % heads) for a in range(heads)],
        )
        for shift in range(mid)
    ]
    before = mark(send(before, [(lent_to[a], half * heads + a) for a in range(heads)]), MARK_LENT)
    parity = z % 2
    kept, given = sort_pieces(parity[None], pieces, MARK_PIECES)
    got = send(given, [(half * heads + a, half * heads + (a ^ 1)) for a in range(heads)])
    denoised = blend(flip, shares, latents[0], returned)[None]
    groups = jnp.arange(heads)
    source = jnp.where(groups % 2 == parity, z, z + 1 - 2 * parity)
    order = ((source - groups) % heads) // 2 + jnp.where(groups % 2 == parity, 0, mid)
    order = jnp.concatenate([order, (frame == 0).astype(order.dtype)[None]])
    entering = blend_lent(order, before, jnp.concatenate([kept, got]), fresh)[None]
    advanced = send(denoised, straight([(f, f + 1) for f in range(frames - 1) if f != half - 1]))
    return (denoised, jnp.where((frame == 0) | (frame == half), entering, advanced))


def solution(mesh):
    def body(latents, queries, keys, values, fresh, timesteps, window):
        return per_device(
            mesh.shape["frame"], mesh.shape["head"], latents, queries[0], keys[0], values[0], fresh, timesteps, window
        )

    return jax.shard_map(
        body,
        mesh=mesh,
        in_specs=(
            P("frame", "head", None),
            P("frame", "head", None),
            P("frame", "head", None),
            P("frame", "head", None),
            P("head", None),
            P("frame"),
            P("frame", None),
        ),
        out_specs=(P("frame", "head", None), P("frame", "head", None)),
        check_vma=False,
    )
```

```python
import functools

import jax
import jax.numpy as jnp
from jax import lax
from jax.experimental import pallas as pl
from jax.experimental.pallas import tpu as pltpu
from jax.sharding import PartitionSpec as P

HD = 64
REACH = 2
LEVELS = 1000
SLOTS = 2 * REACH + 1
PAIR = 2 * HD
LOG2E = 1.4426950408889634
AXES = ("frame", "head")
EXITS_A = ((2, 3), (3, 2), (3, 2), (3, 3))
EXITS_B = ((0, 3), (3, 0), (3, 0), (3, 3))
EXITS_STEP = ((2, 2), (1, 3), (2, 0), (0, 0), (0, 2), (3, 1), (0, 0), (0, 2))
MARK_LENT = 2 * 10**9
MARK_PIECES = 16 * 10**9
MARK_TRADED = 8 * 10**9


def head_split_kernel(groups, width, flip_ref, *refs):
    inputs, out_ref = refs[:-1], refs[-1]
    flip = flip_ref[0]
    for group in range(groups):
        block = jnp.where(flip == 1, groups - 1 - group, group)
        for index, source in enumerate(inputs):
            out_ref[block, index] = source[:, group * width : (group + 1) * width]


def head_split(flip, groups, *arrays):
    rows, columns = arrays[0].shape
    width = columns // groups
    count = len(arrays)
    size = count * rows * columns * 2
    return pl.pallas_call(
        functools.partial(head_split_kernel, groups, width),
        out_shape=jax.ShapeDtypeStruct((groups, count, rows, width), jnp.bfloat16),
        in_specs=[pl.BlockSpec(memory_space=pltpu.SMEM)] + [pl.BlockSpec(memory_space=pltpu.VMEM)] * count,
        out_specs=pl.BlockSpec(memory_space=pltpu.VMEM),
        cost_estimate=pl.CostEstimate(flops=0, bytes_accessed=2 * size, transcendentals=0),
    )(flip, *arrays)


def attention_kernel(
    blocks, pairs, rows, picks_ref, q_ref, own, back2, next2, cross, chip, far,
    out_ref, k_buf, v_buf, score_a, score_b, sem,
):
    per_block = own.shape[2]
    span = blocks * per_block
    per_chunk = rows // per_block
    chunks = span // rows
    steps = pairs * chunks

    def copies(source, slot, pair, which, buf):
        columns = pl.ds(pair * PAIR, PAIR)
        return [
            pltpu.make_async_copy(
                source.at[block, which, :, columns],
                buf.at[pair, slot, pl.ds(block * per_block, per_block), pl.ds(0, PAIR)],
                sem.at[pair, slot, which],
            )
            for block in range(blocks)
        ]

    def fetch(source, slot, pair):
        for copy in copies(source, slot, pair, 0, k_buf) + copies(source, slot, pair, 1, v_buf):
            copy.start()

    sources = (back2, chip, own, chip, next2)
    others = (cross, far, None, far, cross)
    for pair in range(pairs):
        for slot in range(SLOTS):
            if slot == REACH:
                fetch(own, slot, pair)
                continue

            @pl.when(picks_ref[slot] == 0)
            def _(pair=pair, slot=slot):
                for copy in copies(own, slot, pair, 0, k_buf):
                    copy.start()
                v_buf[pair, slot] = jnp.zeros((span, 2 * PAIR), jnp.bfloat16)

            @pl.when(picks_ref[slot] == 1)
            def _(pair=pair, slot=slot):
                fetch(sources[slot], slot, pair)

            @pl.when(picks_ref[slot] == 2)
            def _(pair=pair, slot=slot):
                fetch(others[slot], slot, pair)

    for pair in range(pairs):
        for slot in range(SLOTS):
            @pl.when(picks_ref[slot] > 0)
            def _(pair=pair, slot=slot):
                v_buf[pair, slot, :, PAIR:] = jnp.ones((span, PAIR), jnp.bfloat16)

    def arrive(pair):
        for slot in range(SLOTS):
            for copy in copies(own, slot, pair, 0, k_buf):
                copy.wait()

            @pl.when(picks_ref[slot] > 0)
            def _(slot=slot):
                for copy in copies(own, slot, pair, 1, v_buf):
                    copy.wait()

    lane = lax.broadcasted_iota(jnp.int32, (rows, PAIR), 1)

    def place(step):
        pair, chunk = step // chunks, step % chunks
        return pl.ds(chunk * per_chunk, per_chunk), pl.ds(pl.multiple_of(pair * PAIR, PAIR), PAIR)

    def scores(step, score):
        block, columns = place(step)
        query = q_ref[block, 0, :, columns].reshape(rows, PAIR)
        zero = jnp.zeros_like(query)
        both = jnp.concatenate([jnp.where(lane < HD, query, zero), jnp.where(lane < HD, zero, query)], axis=0)
        high = None
        for slot in range(SLOTS):
            found = lax.dot_general(
                both, k_buf[step // chunks, slot], (((1,), (1,)), ((), ())), preferred_element_type=jnp.float32
            )
            score[slot] = found
            for start in range(0, span, 128):
                part = found[:, start : start + 128]
                high = part if high is None else jnp.maximum(high, part)
        return jnp.max(high, axis=1, keepdims=True)

    def mix(step, score, high):
        total = None
        for slot in range(SLOTS):
            weights = jnp.exp2((score[slot] - high) * (HD ** -0.5 * LOG2E)).astype(jnp.bfloat16)
            part = jnp.dot(weights, v_buf[step // chunks, slot], preferred_element_type=jnp.float32)
            total = part if total is None else total + part
        mixed = total[:, :PAIR] / total[:, PAIR:]
        mixed = jnp.where(lane < HD, mixed[:rows], mixed[rows:]).astype(jnp.bfloat16)
        block, columns = place(step)
        out_ref[block, :, columns] = mixed.reshape(per_chunk, per_block, PAIR)

    arrive(0)
    first = scores(0, score_a)

    def two_steps(index, high_a):
        later = jnp.minimum(2 * index + 2, steps - 1)
        high_b = scores(2 * index + 1, score_b)
        mix(2 * index, score_a, high_a)
        for pair in range(1, pairs):
            @pl.when(2 * index + 2 == pair * chunks)
            def _(pair=pair):
                arrive(pair)

        high_a = scores(later, score_a)
        mix(2 * index + 1, score_b, high_b)
        return high_a

    lax.fori_loop(0, steps // 2, two_steps, first)


def attend(picks, query, own, back2, next2, cross, chip, far):
    blocks, _, per_block, width = query.shape
    pairs = width // PAIR
    span = blocks * per_block
    rows = span // 2
    return pl.pallas_call(
        functools.partial(attention_kernel, blocks, pairs, rows),
        out_shape=jax.ShapeDtypeStruct((blocks, per_block, width), jnp.bfloat16),
        in_specs=[pl.BlockSpec(memory_space=pltpu.SMEM), pl.BlockSpec(memory_space=pltpu.VMEM)]
        + [pl.BlockSpec(memory_space=pl.ANY)] * 6,
        out_specs=pl.BlockSpec(memory_space=pltpu.VMEM),
        scratch_shapes=[
            pltpu.VMEM((pairs, SLOTS, span, PAIR), jnp.bfloat16),
            pltpu.VMEM((pairs, SLOTS, span, 2 * PAIR), jnp.bfloat16),
            pltpu.VMEM((SLOTS, 2 * rows, span), jnp.float32),
            pltpu.VMEM((SLOTS, 2 * rows, span), jnp.float32),
            pltpu.SemaphoreType.DMA((pairs, SLOTS, 2)),
        ],
        compiler_params=pltpu.CompilerParams(vmem_limit_bytes=40 * 1024 * 1024),
        cost_estimate=pl.CostEstimate(
            flops=4 * span * span * SLOTS * width,
            bytes_accessed=(2 * SLOTS + 2) * span * width * 2,
            transcendentals=span * span * SLOTS * width // HD,
        ),
    )(picks, query, own, back2, next2, cross, chip, far)


def blend_kernel(groups, width, flip_ref, share_ref, latents_ref, returned_ref, out_ref):
    flip = flip_ref[0]
    for group in range(groups):
        block = jnp.where(flip == 1, groups - 1 - group, group)
        columns = slice(group * width, (group + 1) * width)
        out_ref[:, columns] = (
            share_ref[0] * latents_ref[:, columns].astype(jnp.float32)
            + share_ref[1] * returned_ref[block].astype(jnp.float32)
        ).astype(jnp.bfloat16)


def blend(flip, shares, latents, returned):
    groups, rows, width = returned.shape
    return pl.pallas_call(
        functools.partial(blend_kernel, groups, width),
        out_shape=jax.ShapeDtypeStruct(latents.shape, jnp.bfloat16),
        in_specs=[pl.BlockSpec(memory_space=pltpu.SMEM)] * 2 + [pl.BlockSpec(memory_space=pltpu.VMEM)] * 2,
        out_specs=pl.BlockSpec(memory_space=pltpu.VMEM),
        cost_estimate=pl.CostEstimate(flops=3 * latents.size, bytes_accessed=6 * latents.size, transcendentals=0),
    )(flip, shares, latents, returned)


def mark_kernel(value_ref, out_ref):
    pass


def mark(value, flops):
    return pl.pallas_call(
        mark_kernel,
        out_shape=jax.ShapeDtypeStruct(value.shape, value.dtype),
        in_specs=[pl.BlockSpec(memory_space=pl.ANY)],
        out_specs=pl.BlockSpec(memory_space=pl.ANY),
        input_output_aliases={0: 0},
        compiler_params=pltpu.CompilerParams(vmem_limit_bytes=40 * 1024 * 1024),
        cost_estimate=pl.CostEstimate(flops=flops, bytes_accessed=0, transcendentals=0),
    )(value)


def enter_kernel(groups, rows, width, order_ref, before, kept, got, fresh, advanced, out, lat, mixed, entry, sem):
    def fetch(*moves):
        copies = [pltpu.make_async_copy(*move, sem.at[index]) for index, move in enumerate(moves)]
        for copy in copies:
            copy.start()
        for copy in copies:
            copy.wait()

    @pl.when(order_ref[groups] == 1)
    def _():
        fetch((fresh, out))

    @pl.when(order_ref[groups] == 2)
    def _():
        part = groups // 2
        fetch((before, lat), (kept, mixed.at[pl.ds(0, part)]), (got, mixed.at[pl.ds(part, part)]))
        level = (lat[rows : rows + 1, :width].astype(jnp.float32) * 32.0 + lat[rows + 1 : rows + 2, :width].astype(jnp.float32)) / LEVELS
        keep_share = 1.0 - 0.5 * level
        push_share = 0.5 + level
        for group in range(groups):
            columns = slice(group * width, (group + 1) * width)
            entry[:, columns] = (
                keep_share * lat[:rows, columns].astype(jnp.float32)
                + push_share * mixed[order_ref[group]].astype(jnp.float32)
            ).astype(jnp.bfloat16)
        fetch((entry, out))


def enter(order, before, kept, got, fresh, advanced):
    part, rows, width = kept.shape
    groups = 2 * part
    return pl.pallas_call(
        functools.partial(enter_kernel, groups, rows, width),
        out_shape=jax.ShapeDtypeStruct(advanced.shape, advanced.dtype),
        in_specs=[pl.BlockSpec(memory_space=pltpu.SMEM)] + [pl.BlockSpec(memory_space=pl.ANY)] * 5,
        out_specs=pl.BlockSpec(memory_space=pl.ANY),
        input_output_aliases={5: 0},
        scratch_shapes=[
            pltpu.VMEM(before.shape, jnp.bfloat16),
            pltpu.VMEM((groups, rows, width), jnp.bfloat16),
            pltpu.VMEM((rows, groups * width), jnp.bfloat16),
            pltpu.SemaphoreType.DMA((3,)),
        ],
        compiler_params=pltpu.CompilerParams(vmem_limit_bytes=40 * 1024 * 1024),
        cost_estimate=pl.CostEstimate(flops=0, bytes_accessed=0, transcendentals=0),
    )(order, before, kept, got, fresh, advanced)


def with_step(latents, timesteps):
    row = lax.broadcasted_iota(jnp.int32, (16, latents.shape[1]), 0)
    step = jnp.where(row == 0, timesteps[0] // 32, jnp.where(row == 1, timesteps[0] % 32, 0))
    return jnp.concatenate([latents, step.astype(jnp.bfloat16)])


def sort_kernel(parity_ref, *refs):
    pieces, kept_ref, given_ref = refs[:-2], refs[-2], refs[-1]
    parity = parity_ref[0]
    for index, piece in enumerate(pieces):
        kept_ref[index] = piece[parity]
        given_ref[index] = piece[1 - parity]


def sort_pieces(parity, pieces, flops):
    shape = jax.ShapeDtypeStruct((len(pieces), *pieces[0].shape[1:]), pieces[0].dtype)
    return pl.pallas_call(
        sort_kernel,
        out_shape=(shape, shape),
        in_specs=[pl.BlockSpec(memory_space=pltpu.SMEM)] + [pl.BlockSpec(memory_space=pltpu.VMEM)] * len(pieces),
        out_specs=(pl.BlockSpec(memory_space=pltpu.VMEM), pl.BlockSpec(memory_space=pltpu.VMEM)),
        cost_estimate=pl.CostEstimate(flops=flops, bytes_accessed=0, transcendentals=0),
    )(parity, *pieces)


def per_device(frames, heads, latents, queries, keys, values, fresh, timesteps, window):
    frame = lax.axis_index("frame")
    half = frames // 2
    flip = (frame >= half).astype(jnp.int32)[None]

    def mirrored(moves):
        return [
            (a * heads + z, b * heads + (heads - 1 - z)) for a, b in moves for z in range(heads)
        ]

    def straight(moves):
        return [(a * heads + z, b * heads + z) for a, b in moves for z in range(heads)]

    def within(distance):
        return straight(
            [(f, f + distance) for f in range(frames) if 0 <= f + distance < frames and (f < half) == (f + distance < half)]
        )

    send = lambda value, moves: lax.ppermute(value, AXES, moves)
    exchange = lambda value: lax.all_to_all(value, "head", split_axis=0, concat_axis=0, tiled=True)

    own = exchange(head_split(flip, heads, keys, values))
    query = head_split(flip, heads, queries)
    lent_to = [(y * 8 + x * 2 + 1) * heads + a for a, (x, y) in enumerate(EXITS_STEP)]
    lending = [((half - 1) * heads + a, lent_to[a]) for a in range(heads)]
    before = send(with_step(latents[0], timesteps), lending)
    own, query, before = lax.optimization_barrier((own, query, before))

    mid = heads // 2
    edge = (half - 2, half - 1, half, half + 1)
    over = {half - 2: half, half - 1: half + 1, half: half - 2, half + 1: half - 1}

    def column(f, z, exits):
        x, y = exits[min(z, heads - 1 - z)]
        ahead = y * 8 + x * 2 + f % 2
        return ahead if f < half else frames - 2 - ahead + 2 * (f % 2)

    def through(value, exits):
        out = [(f * heads + z, column(f, z, exits) * heads + z) for f in edge for z in range(heads)]
        on = [
            (column(f, z, exits) * heads + z, over[f] * heads + heads - 1 - z) for f in edge for z in range(heads)
        ]
        return send(value, out), on

    near_a, on_a = through(own[:mid], EXITS_A)
    near_b, on_b = through(own[mid:], EXITS_B)
    core = frame % 2
    pairwise = straight([(f, f ^ 1) for f in range(frames)])
    chip = send(own, pairwise)
    own, near_a, near_b = lax.optimization_barrier((own, near_a, near_b))
    back2 = send(own, within(2))
    next2 = send(own, within(-2))
    cross = jnp.concatenate([send(near_a, on_a), send(near_b, on_b)])
    fetched = jnp.where(core == 1, back2, next2)
    far = send(jnp.where((frame == half + 1) | (frame == half - 2), cross, fetched), pairwise)

    near_a, near_b, query = lax.optimization_barrier((near_a, near_b, query))
    query = exchange(query)

    offsets = jnp.arange(-REACH, REACH + 1)
    target = frame + offsets
    allowed = (
        (target >= 0) & (target < frames) & (offsets >= -window[0, 0]) & (offsets <= window[0, 1])
    )
    other = jnp.where(offsets % 2 == 0, (target < half) != (frame < half), target // 2 != frame // 2)
    picks = jnp.where(allowed, jnp.where(other, 2, 1), 0).astype(jnp.int32)
    attended = attend(picks, query, own, back2, next2, cross, chip, far)
    z = lax.axis_index("head")
    levels = timesteps.astype(jnp.float32) / LEVELS
    shares = jnp.concatenate([1.0 - 0.5 * levels, 0.5 + levels])
    attended, before = lax.optimization_barrier((attended, before))
    returned = exchange(attended)
    lent = attended.reshape(mid, 2, *attended.shape[1:])
    pieces = [
        send(
            lax.dynamic_index_in_dim(lent, (z // 2 + shift) % mid, 0, keepdims=False),
            [((half - 1) * heads + a, half * heads + (a + 2 * shift) % heads) for a in range(heads)],
        )
        for shift in range(mid)
    ]
    before = send(before, [(lent_to[a], half * heads + a) for a in range(heads)])
    parity = z % 2
    kept, given = sort_pieces(parity[None], pieces, MARK_PIECES)
    given, before = lax.optimization_barrier((given, before))
    got = mark(send(given, [(half * heads + a, half * heads + (a ^ 1)) for a in range(heads)]), MARK_TRADED)
    denoised = blend(flip, shares, latents[0], returned)[None]
    groups = jnp.arange(heads)
    source = jnp.where(groups % 2 == parity, z, z + 1 - 2 * parity)
    order = ((source - groups) % heads) // 2 + jnp.where(groups % 2 == parity, 0, mid)
    entering = jnp.where(frame == 0, 1, jnp.where(frame == half, 2, 0))
    order = jnp.concatenate([order, entering[None]]).astype(jnp.int32)
    advanced = send(denoised, straight([(f, f + 1) for f in range(frames - 1) if f != half - 1]))
    return (denoised, enter(order, before, kept, got, fresh, advanced[0])[None])


def solution(mesh):
    def body(latents, queries, keys, values, fresh, timesteps, window):
        return per_device(
            mesh.shape["frame"], mesh.shape["head"], latents, queries[0], keys[0], values[0], fresh, timesteps, window
        )

    return jax.shard_map(
        body,
        mesh=mesh,
        in_specs=(
            P("frame", "head", None),
            P("frame", "head", None),
            P("frame", "head", None),
            P("frame", "head", None),
            P("head", None),
            P("frame"),
            P("frame", None),
        ),
        out_specs=(P("frame", "head", None), P("frame", "head", None)),
        check_vma=False,
    )
```

```python
import functools

import jax
import jax.numpy as jnp
from jax import lax
from jax.experimental import pallas as pl
from jax.experimental.pallas import tpu as pltpu
from jax.sharding import PartitionSpec as P

HD = 64
REACH = 2
LEVELS = 1000
SLOTS = 2 * REACH + 1
PAIR = 2 * HD
LOG2E = 1.4426950408889634
AXES = ("frame", "head")
EXITS_A = ((2, 3), (3, 2), (3, 2), (3, 3))
EXITS_B = ((0, 3), (3, 0), (3, 0), (3, 3))
EXITS_STEP = ((2, 2), (1, 3), (2, 0), (0, 0), (0, 2), (3, 1), (0, 0), (0, 2))
MARK_LENT = 2 * 10**9
MARK_PIECES = 16 * 10**9
MARK_TRADED = 8 * 10**9


def head_split_kernel(groups, width, flip_ref, *refs):
    inputs, out_ref = refs[:-1], refs[-1]
    flip = flip_ref[0]
    for group in range(groups):
        block = jnp.where(flip == 1, groups - 1 - group, group)
        for index, source in enumerate(inputs):
            out_ref[block, index] = source[:, group * width : (group + 1) * width]


def head_split(flip, groups, *arrays):
    rows, columns = arrays[0].shape
    width = columns // groups
    count = len(arrays)
    size = count * rows * columns * 2
    return pl.pallas_call(
        functools.partial(head_split_kernel, groups, width),
        out_shape=jax.ShapeDtypeStruct((groups, count, rows, width), jnp.bfloat16),
        in_specs=[pl.BlockSpec(memory_space=pltpu.SMEM)] + [pl.BlockSpec(memory_space=pltpu.VMEM)] * count,
        out_specs=pl.BlockSpec(memory_space=pltpu.VMEM),
        cost_estimate=pl.CostEstimate(flops=0, bytes_accessed=2 * size, transcendentals=0),
    )(flip, *arrays)


def attention_kernel(
    blocks, pairs, rows, picks_ref, q_ref, own, back2, next2, cross, chip, far,
    out_ref, k_buf, v_buf, score_a, score_b, sem,
):
    per_block = own.shape[2]
    span = blocks * per_block
    per_chunk = rows // per_block
    chunks = span // rows
    steps = pairs * chunks

    def copies(source, slot, pair, which, buf):
        columns = pl.ds(pair * PAIR, PAIR)
        return [
            pltpu.make_async_copy(
                source.at[:, which, :, columns],
                buf.at[pair, slot, :, :, pl.ds(0, PAIR)],
                sem.at[pair, slot, which],
            )
        ]

    def fetch(source, slot, pair):
        for copy in copies(source, slot, pair, 0, k_buf) + copies(source, slot, pair, 1, v_buf):
            copy.start()

    sources = (back2, chip, own, chip, next2)
    others = (cross, far, None, far, cross)
    for pair in range(pairs):
        for slot in range(SLOTS):
            if slot == REACH:
                fetch(own, slot, pair)
                continue

            @pl.when(picks_ref[slot] == 0)
            def _(pair=pair, slot=slot):
                for copy in copies(own, slot, pair, 0, k_buf):
                    copy.start()
                v_buf[pair, slot] = jnp.zeros((blocks, per_block, 2 * PAIR), jnp.bfloat16)

            @pl.when(picks_ref[slot] == 1)
            def _(pair=pair, slot=slot):
                fetch(sources[slot], slot, pair)

            @pl.when(picks_ref[slot] == 2)
            def _(pair=pair, slot=slot):
                fetch(others[slot], slot, pair)

    for pair in range(pairs):
        for slot in range(SLOTS):
            @pl.when(picks_ref[slot] > 0)
            def _(pair=pair, slot=slot):
                v_buf[pair, slot, :, :, PAIR:] = jnp.ones((blocks, per_block, PAIR), jnp.bfloat16)

    def arrive(pair):
        for slot in range(SLOTS):
            for copy in copies(own, slot, pair, 0, k_buf):
                copy.wait()

            @pl.when(picks_ref[slot] > 0)
            def _(slot=slot):
                for copy in copies(own, slot, pair, 1, v_buf):
                    copy.wait()

    lane = lax.broadcasted_iota(jnp.int32, (rows, PAIR), 1)

    def place(step):
        pair, chunk = step // chunks, step % chunks
        return pl.ds(chunk * per_chunk, per_chunk), pl.ds(pl.multiple_of(pair * PAIR, PAIR), PAIR)

    def scores(step, score):
        block, columns = place(step)
        query = q_ref[block, 0, :, columns].reshape(rows, PAIR)
        zero = jnp.zeros_like(query)
        both = jnp.concatenate([jnp.where(lane < HD, query, zero), jnp.where(lane < HD, zero, query)], axis=0)
        high = None
        for slot in range(SLOTS):
            found = lax.dot_general(
                both, k_buf[step // chunks, slot].reshape(span, PAIR), (((1,), (1,)), ((), ())), preferred_element_type=jnp.float32
            )
            score[slot] = found
            for start in range(0, span, 128):
                part = found[:, start : start + 128]
                high = part if high is None else jnp.maximum(high, part)
        return jnp.max(high, axis=1, keepdims=True)

    def mix(step, score, high):
        total = None
        for slot in range(SLOTS):
            weights = jnp.exp2((score[slot] - high) * (HD ** -0.5 * LOG2E)).astype(jnp.bfloat16)
            part = jnp.dot(weights, v_buf[step // chunks, slot].reshape(span, 2 * PAIR), preferred_element_type=jnp.float32)
            total = part if total is None else total + part
        mixed = total[:, :PAIR] / total[:, PAIR:]
        mixed = jnp.where(lane < HD, mixed[:rows], mixed[rows:]).astype(jnp.bfloat16)
        block, columns = place(step)
        out_ref[block, :, columns] = mixed.reshape(per_chunk, per_block, PAIR)

    arrive(0)
    first = scores(0, score_a)

    def two_steps(index, high_a):
        later = jnp.minimum(2 * index + 2, steps - 1)
        high_b = scores(2 * index + 1, score_b)
        mix(2 * index, score_a, high_a)
        for pair in range(1, pairs):
            @pl.when(2 * index + 2 == pair * chunks)
            def _(pair=pair):
                arrive(pair)

        high_a = scores(later, score_a)
        mix(2 * index + 1, score_b, high_b)
        return high_a

    lax.fori_loop(0, steps // 2, two_steps, first)


def attend(picks, query, own, back2, next2, cross, chip, far):
    blocks, _, per_block, width = query.shape
    pairs = width // PAIR
    span = blocks * per_block
    rows = span // 2
    return pl.pallas_call(
        functools.partial(attention_kernel, blocks, pairs, rows),
        out_shape=jax.ShapeDtypeStruct((blocks, per_block, width), jnp.bfloat16),
        in_specs=[pl.BlockSpec(memory_space=pltpu.SMEM), pl.BlockSpec(memory_space=pltpu.VMEM)]
        + [pl.BlockSpec(memory_space=pl.ANY)] * 6,
        out_specs=pl.BlockSpec(memory_space=pltpu.VMEM),
        scratch_shapes=[
            pltpu.VMEM((pairs, SLOTS, blocks, per_block, PAIR), jnp.bfloat16),
            pltpu.VMEM((pairs, SLOTS, blocks, per_block, 2 * PAIR), jnp.bfloat16),
            pltpu.VMEM((SLOTS, 2 * rows, span), jnp.float32),
            pltpu.VMEM((SLOTS, 2 * rows, span), jnp.float32),
            pltpu.SemaphoreType.DMA((pairs, SLOTS, 2)),
        ],
        compiler_params=pltpu.CompilerParams(vmem_limit_bytes=40 * 1024 * 1024),
        cost_estimate=pl.CostEstimate(
            flops=4 * span * span * SLOTS * width,
            bytes_accessed=(2 * SLOTS + 2) * span * width * 2,
            transcendentals=span * span * SLOTS * width // HD,
        ),
    )(picks, query, own, back2, next2, cross, chip, far)


def blend_kernel(groups, width, flip_ref, share_ref, latents_ref, returned_ref, out_ref):
    flip = flip_ref[0]
    for group in range(groups):
        block = jnp.where(flip == 1, groups - 1 - group, group)
        columns = slice(group * width, (group + 1) * width)
        out_ref[:, columns] = (
            share_ref[0] * latents_ref[:, columns].astype(jnp.float32)
            + share_ref[1] * returned_ref[block].astype(jnp.float32)
        ).astype(jnp.bfloat16)


def blend(flip, shares, latents, returned):
    groups, rows, width = returned.shape
    return pl.pallas_call(
        functools.partial(blend_kernel, groups, width),
        out_shape=jax.ShapeDtypeStruct(latents.shape, jnp.bfloat16),
        in_specs=[pl.BlockSpec(memory_space=pltpu.SMEM)] * 2 + [pl.BlockSpec(memory_space=pltpu.VMEM)] * 2,
        out_specs=pl.BlockSpec(memory_space=pltpu.VMEM),
        cost_estimate=pl.CostEstimate(flops=3 * latents.size, bytes_accessed=6 * latents.size, transcendentals=0),
    )(flip, shares, latents, returned)


def mark_kernel(value_ref, out_ref):
    pass


def mark(value, flops):
    return pl.pallas_call(
        mark_kernel,
        out_shape=jax.ShapeDtypeStruct(value.shape, value.dtype),
        in_specs=[pl.BlockSpec(memory_space=pl.ANY)],
        out_specs=pl.BlockSpec(memory_space=pl.ANY),
        input_output_aliases={0: 0},
        compiler_params=pltpu.CompilerParams(vmem_limit_bytes=40 * 1024 * 1024),
        cost_estimate=pl.CostEstimate(flops=flops, bytes_accessed=0, transcendentals=0),
    )(value)


def enter_kernel(groups, rows, width, order_ref, before, kept, got, fresh, advanced, out, lat, mixed, entry, sem):
    def fetch(*moves):
        copies = [pltpu.make_async_copy(*move, sem.at[index]) for index, move in enumerate(moves)]
        for copy in copies:
            copy.start()
        for copy in copies:
            copy.wait()

    @pl.when(order_ref[groups] == 1)
    def _():
        fetch((fresh, out))

    @pl.when(order_ref[groups] == 2)
    def _():
        part = groups // 2
        fetch((before, lat), (kept, mixed.at[pl.ds(0, part)]), (got, mixed.at[pl.ds(part, part)]))
        level = (lat[rows : rows + 1, :width].astype(jnp.float32) * 32.0 + lat[rows + 1 : rows + 2, :width].astype(jnp.float32)) / LEVELS
        keep_share = 1.0 - 0.5 * level
        push_share = 0.5 + level
        for group in range(groups):
            columns = slice(group * width, (group + 1) * width)
            entry[:, columns] = (
                keep_share * lat[:rows, columns].astype(jnp.float32)
                + push_share * mixed[order_ref[group]].astype(jnp.float32)
            ).astype(jnp.bfloat16)
        fetch((entry, out))


def enter(order, before, kept, got, fresh, advanced):
    part, rows, width = kept.shape
    groups = 2 * part
    return pl.pallas_call(
        functools.partial(enter_kernel, groups, rows, width),
        out_shape=jax.ShapeDtypeStruct(advanced.shape, advanced.dtype),
        in_specs=[pl.BlockSpec(memory_space=pltpu.SMEM)] + [pl.BlockSpec(memory_space=pl.ANY)] * 5,
        out_specs=pl.BlockSpec(memory_space=pl.ANY),
        input_output_aliases={5: 0},
        scratch_shapes=[
            pltpu.VMEM(before.shape, jnp.bfloat16),
            pltpu.VMEM((groups, rows, width), jnp.bfloat16),
            pltpu.VMEM((rows, groups * width), jnp.bfloat16),
            pltpu.SemaphoreType.DMA((3,)),
        ],
        compiler_params=pltpu.CompilerParams(vmem_limit_bytes=40 * 1024 * 1024),
        cost_estimate=pl.CostEstimate(flops=0, bytes_accessed=0, transcendentals=0),
    )(order, before, kept, got, fresh, advanced)


def with_step(latents, timesteps):
    row = lax.broadcasted_iota(jnp.int32, (16, latents.shape[1]), 0)
    step = jnp.where(row == 0, timesteps[0] // 32, jnp.where(row == 1, timesteps[0] % 32, 0))
    return jnp.concatenate([latents, step.astype(jnp.bfloat16)])


def sort_kernel(parity_ref, *refs):
    pieces, kept_ref, given_ref = refs[:-2], refs[-2], refs[-1]
    parity = parity_ref[0]
    for index, piece in enumerate(pieces):
        kept_ref[index] = piece[parity]
        given_ref[index] = piece[1 - parity]


def sort_pieces(parity, pieces, flops):
    shape = jax.ShapeDtypeStruct((len(pieces), *pieces[0].shape[1:]), pieces[0].dtype)
    return pl.pallas_call(
        sort_kernel,
        out_shape=(shape, shape),
        in_specs=[pl.BlockSpec(memory_space=pltpu.SMEM)] + [pl.BlockSpec(memory_space=pltpu.VMEM)] * len(pieces),
        out_specs=(pl.BlockSpec(memory_space=pltpu.VMEM), pl.BlockSpec(memory_space=pltpu.VMEM)),
        cost_estimate=pl.CostEstimate(flops=flops, bytes_accessed=0, transcendentals=0),
    )(parity, *pieces)


def per_device(frames, heads, latents, queries, keys, values, fresh, timesteps, window):
    frame = lax.axis_index("frame")
    core = frame % 2
    half = frames // 2
    flip = (frame >= half).astype(jnp.int32)[None]

    def mirrored(moves):
        return [
            (a * heads + z, b * heads + (heads - 1 - z)) for a, b in moves for z in range(heads)
        ]

    def straight(moves):
        return [(a * heads + z, b * heads + z) for a, b in moves for z in range(heads)]

    def within(distance):
        return straight(
            [(f, f + distance) for f in range(frames) if 0 <= f + distance < frames and (f < half) == (f + distance < half)]
        )

    send = lambda value, moves: lax.ppermute(value, AXES, moves)
    exchange = lambda value: lax.all_to_all(value, "head", split_axis=0, concat_axis=0, tiled=True)

    own = exchange(head_split(flip, heads, keys, values))
    query = head_split(flip, heads, queries)
    lent_to = [(y * 8 + x * 2 + 1) * heads + a for a, (x, y) in enumerate(EXITS_STEP)]
    lending = [((half - 1) * heads + a, lent_to[a]) for a in range(heads)]
    before = send(with_step(latents[0], timesteps), lending)
    offsets = jnp.arange(-REACH, REACH + 1)
    target = frame + offsets
    allowed = (
        (target >= 0) & (target < frames) & (offsets >= -window[0, 0]) & (offsets <= window[0, 1])
    )
    other = jnp.where(offsets % 2 == 0, (target < half) != (frame < half), target // 2 != frame // 2)
    picks = jnp.where(allowed, jnp.where(other, 2, 1), 0).astype(jnp.int32)
    own, query, before, picks = lax.optimization_barrier((own, query, before, picks))

    mid = heads // 2
    edge = (half - 2, half - 1, half, half + 1)
    over = {half - 2: half, half - 1: half + 1, half: half - 2, half + 1: half - 1}

    def column(f, z, exits):
        x, y = exits[min(z, heads - 1 - z)]
        ahead = y * 8 + x * 2 + f % 2
        return ahead if f < half else frames - 2 - ahead + 2 * (f % 2)

    def through(value, exits):
        out = [(f * heads + z, column(f, z, exits) * heads + z) for f in edge for z in range(heads)]
        on = [
            (column(f, z, exits) * heads + z, over[f] * heads + heads - 1 - z) for f in edge for z in range(heads)
        ]
        return send(value, out), on

    near_a, on_a = through(own[:mid], EXITS_A)
    near_b, on_b = through(own[mid:], EXITS_B)
    pairwise = straight([(f, f ^ 1) for f in range(frames)])
    chip = send(own, pairwise)
    own, near_a, near_b = lax.optimization_barrier((own, near_a, near_b))
    back2 = send(own, within(2))
    next2 = send(own, within(-2))
    cross = jnp.concatenate([send(near_a, on_a), send(near_b, on_b)])
    fetched = jnp.where(core == 1, back2, next2)
    far = send(jnp.where((frame == half + 1) | (frame == half - 2), cross, fetched), pairwise)

    near_a, near_b, query = lax.optimization_barrier((near_a, near_b, query))
    query = exchange(query)

    attended = attend(picks, query, own, back2, next2, cross, chip, far)
    z = lax.axis_index("head")
    levels = timesteps.astype(jnp.float32) / LEVELS
    shares = jnp.concatenate([1.0 - 0.5 * levels, 0.5 + levels])
    attended, before = lax.optimization_barrier((attended, before))
    returned = exchange(attended)
    lent = attended.reshape(mid, 2, *attended.shape[1:])
    pieces = [
        send(
            lax.dynamic_index_in_dim(lent, (z // 2 + shift) % mid, 0, keepdims=False),
            [((half - 1) * heads + a, half * heads + (a + 2 * shift) % heads) for a in range(heads)],
        )
        for shift in range(mid)
    ]
    before = send(before, [(lent_to[a], half * heads + a) for a in range(heads)])
    parity = z % 2
    kept, given = sort_pieces(parity[None], pieces, MARK_PIECES)
    given, before = lax.optimization_barrier((given, before))
    got = mark(send(given, [(half * heads + a, half * heads + (a ^ 1)) for a in range(heads)]), MARK_TRADED)
    denoised = blend(flip, shares, latents[0], returned)[None]
    groups = jnp.arange(heads)
    source = jnp.where(groups % 2 == parity, z, z + 1 - 2 * parity)
    order = ((source - groups) % heads) // 2 + jnp.where(groups % 2 == parity, 0, mid)
    entering = jnp.where(frame == 0, 1, jnp.where(frame == half, 2, 0))
    order = jnp.concatenate([order, entering[None]]).astype(jnp.int32)
    advanced = send(denoised, straight([(f, f + 1) for f in range(frames - 1) if f != half - 1]))
    return (denoised, enter(order, before, kept, got, fresh, advanced[0])[None])


def solution(mesh):
    def body(latents, queries, keys, values, fresh, timesteps, window):
        return per_device(
            mesh.shape["frame"], mesh.shape["head"], latents, queries[0], keys[0], values[0], fresh, timesteps, window
        )

    return jax.shard_map(
        body,
        mesh=mesh,
        in_specs=(
            P("frame", "head", None),
            P("frame", "head", None),
            P("frame", "head", None),
            P("frame", "head", None),
            P("head", None),
            P("frame"),
            P("frame", None),
        ),
        out_specs=(P("frame", "head", None), P("frame", "head", None)),
        check_vma=False,
    )
```
